32 devices in a mesh: row: 4 (over y, x), col: 8 (over z, core).
Axes of the slice: x: 2, y: 2, z: 4, core: 2. Of those that a mesh axis runs over, the one named last changes fastest.
Arguments:
- tokens: bfloat16 [384, 8192], P('row', 'col'), may hold values from -6 to 6
- weight_in: bfloat16 [8192, 32768], P('col', 'row'), may hold values from -0.125 to 0.125
- mask_in: int32 [64, 256], P('col', 'row'), may hold values 0 or 1
- weight_out: bfloat16 [32768, 8192], P('row', 'col'), may hold values from -0.0625 to 0.0625
- mask_out: int32 [256, 64], P('row', 'col'), may hold values 0 or 1
- cotangent: bfloat16 [384, 8192], P('row', 'col'), may hold values from -6 to 6
Outputs:
- result: bfloat16 [384, 8192], P('row', 'col')
- tokens_grad: bfloat16 [384, 8192], P('row', 'col')
- weight_in_grad: bfloat16 [8192, 32768], P('col', 'row')
- weight_out_grad: bfloat16 [32768, 8192], P('row', 'col')
The draws below stay inside these ranges and needn't reach their ends.
All inputs are finite; a program needn't handle non-finite values. No bound on the sum of `mask_in` or of `mask_out` on one device may be relied on, other than what follows from the above.
Results may differ from the reference program's by a relative error of at most 0.005.
Values may be sent and summed in bfloat16 or wider, within the bound.
No kernel may reach another device: no remote copies, remote signals or barrier semaphores. Data moves between devices by JAX's collectives and lax.ppermute only.
A program may use at most 192 MiB of HBM per device.

```python
import jax
import jax.numpy as jnp

D = 8192
FF = 32768
BLOCK = 128
TOKENS = 384


def set_ends(drawn, stream_key, least, high):
    spot = [jax.random.randint(jax.random.fold_in(stream_key, axis), (), 0, length) for axis, length in enumerate(drawn.shape)]
    widest = drawn.shape.index(max(drawn.shape))
    next_to = spot[:widest] + [(spot[widest] + 1) % drawn.shape[widest]] + spot[widest + 1:]
    return drawn.at[tuple(spot)].set(least).at[tuple(next_to)].set(high)


def levels(own_key, shape, cuts, low, largest):
    loudness, own = 1.0, jax.random.fold_in(own_key, 6)
    for axis_at, parts in cuts:
        heights = jnp.exp(jax.random.uniform(jax.random.fold_in(own, axis_at), (parts,), jnp.float32, low / len(cuts), largest / len(cuts)))
        loudness = loudness * jnp.repeat(heights, shape[axis_at] // parts).reshape([-1 if axis == axis_at else 1 for axis in range(len(shape))])
    return loudness


def gaussian(own_key, dims, deviation, most, split=(), dtype=jnp.bfloat16):
    values = deviation * jax.random.normal(own_key, dims, jnp.float32)
    if split:
        values = values * levels(own_key, dims, split, -0.22, 0.18)
    return jnp.clip(values, -most, most).astype(dtype)


def setup_inputs(seed: int = 0) -> dict:
    key_list = jax.random.split(jax.random.key(seed), 7)
    tokens = gaussian(key_list[0], (TOKENS, D), 1.0, 6.0, ((0, 4), (1, 8)))
    weight_in = gaussian(key_list[1], (D, FF), (D // 4) ** -0.5, 0.125, ((0, 8), (1, 4)))
    mask_in = set_ends((jax.random.randint(key_list[2], (D // BLOCK, FF // BLOCK), 0, 4) < 1).astype(jnp.int32), jax.random.fold_in(key_list[2], 1), 0, 1)
    weight_out = gaussian(key_list[3], (FF, D), (FF // 4) ** -0.5, 0.0625, ((0, 4), (1, 8)))
    mask_out = set_ends((jax.random.randint(key_list[4], (FF // BLOCK, D // BLOCK), 0, 4) < 1).astype(jnp.int32), jax.random.fold_in(key_list[4], 1), 0, 1)
    cotangent = gaussian(key_list[5], (TOKENS, D), 1.0, 6.0, ((0, 4), (1, 8)))
    return dict(tokens=tokens, weight_in=weight_in, mask_in=mask_in, weight_out=weight_out, mask_out=mask_out, cotangent=cotangent)


root_two_pi = 0.7978845608
cubic_coef = 0.044715


def expand(mask):
    blocks_a, blocks_b = mask.shape
    spread = mask.astype(jnp.bfloat16)
    return jnp.broadcast_to(spread[:, None, :, None], (blocks_a, BLOCK, blocks_b, BLOCK)).reshape(blocks_a * BLOCK, blocks_b * BLOCK)


def gelu_value(values):
    tangent = jnp.tanh(root_two_pi * (values + cubic_coef * values * values * values))
    return 0.5 * values * (1.0 + tangent)


def gelu_slope(values):
    tangent = jnp.tanh(root_two_pi * (values + cubic_coef * values * values * values))
    return 0.5 * (1.0 + tangent) + 0.5 * values * (1.0 - tangent * tangent) * root_two_pi * (1.0 + 3.0 * cubic_coef * values * values)


def reference(tokens, weight_in, mask_in, weight_out, mask_out, cotangent):
    block_in = expand(mask_in)
    block_out = expand(mask_out)
    masked_in = weight_in * block_in
    masked_out = weight_out * block_out
    preact = jnp.dot(tokens, masked_in, preferred_element_type=jnp.float32)
    hidden = gelu_value(preact).astype(jnp.bfloat16)
    result = jnp.dot(hidden, masked_out, preferred_element_type=jnp.float32).astype(jnp.bfloat16)
    hidden_grad = jnp.dot(cotangent, masked_out.T, preferred_element_type=jnp.float32)
    preact_grad = (hidden_grad * gelu_slope(preact)).astype(jnp.bfloat16)
    tokens_grad = jnp.dot(preact_grad, masked_in.T, preferred_element_type=jnp.float32).astype(jnp.bfloat16)
    weight_in_grad = (jnp.dot(tokens.T, preact_grad, preferred_element_type=jnp.float32) * block_in).astype(jnp.bfloat16)
    weight_out_grad = (jnp.dot(hidden.T, cotangent, preferred_element_type=jnp.float32) * block_out).astype(jnp.bfloat16)
    return result, tokens_grad, weight_in_grad, weight_out_grad
```

```python
import functools

import jax
import jax.numpy as jnp
from jax import lax
from jax.experimental import pallas as pl
from jax.experimental.pallas import tpu as pltpu
from jax.sharding import PartitionSpec as P

BLOCK = 128
CHUNKS = 4
VMEM_LIMIT = 40 * 1024 * 1024

root_two_pi = 0.7978845608
cubic_coef = 0.044715


def gelu_value(values):
    tangent = jnp.tanh(root_two_pi * (values + cubic_coef * values * values * values))
    return 0.5 * values * (1.0 + tangent)


def gelu_slope(values):
    tangent = jnp.tanh(root_two_pi * (values + cubic_coef * values * values * values))
    return 0.5 * (1.0 + tangent) + 0.5 * values * (1.0 - tangent * tangent) * root_two_pi * (
        1.0 + 3.0 * cubic_coef * values * values
    )


def contract(left, right, left_dim, right_dim):
    return lax.dot_general(
        left, right, (((left_dim,), (right_dim,)), ((), ())), preferred_element_type=jnp.float32
    )


def masked_block(w_ref, mask_ref, row0, col0):
    rows, cols = w_ref.shape
    bands = []
    for i in range(rows // BLOCK):
        parts = []
        for j in range(cols // BLOCK):
            part = w_ref[i * BLOCK : (i + 1) * BLOCK, j * BLOCK : (j + 1) * BLOCK]
            parts.append(jnp.where(mask_ref[row0 + i, col0 + j] > 0, part, jnp.zeros_like(part)))
        bands.append(parts[0] if len(parts) == 1 else jnp.concatenate(parts, axis=1))
    return bands[0] if len(bands) == 1 else jnp.concatenate(bands, axis=0)


def partial_kernel(transposed, wi, place, mask, x_ref, w_ref, *rest):
    out_ref = rest[-1]
    at = place[pl.program_id(0)] * (wi // BLOCK)
    if transposed:
        term = contract(x_ref[...], masked_block(w_ref, mask, at, 0), 1, 1)
    else:
        term = contract(x_ref[...], masked_block(w_ref, mask, 0, at), 1, 0)
    if len(rest) > 1:
        term += rest[0][0]
    out_ref[0] = term


def partial_sums(x, weight, mask, place, wi, transposed, more=None):
    tokens, depth = x.shape
    if transposed:
        wspec = pl.BlockSpec((wi, depth), lambda d, place, mask: (place[d], 0))
    else:
        wspec = pl.BlockSpec((depth, wi), lambda d, place, mask: (0, place[d]))
    out_spec = pl.BlockSpec((1, tokens, wi), lambda d, place, mask: (d, 0, 0))
    return pl.pallas_call(
        functools.partial(partial_kernel, transposed, wi),
        grid_spec=pltpu.PrefetchScalarGridSpec(
            num_scalar_prefetch=2,
            grid=(2,),
            in_specs=[pl.BlockSpec((tokens, depth), lambda d, place, mask: (0, 0)), wspec] + [out_spec] * (more is not None),
            out_specs=out_spec,
        ),
        out_shape=jax.ShapeDtypeStruct((2, tokens, wi), jnp.float32),
        compiler_params=pltpu.CompilerParams(vmem_limit_bytes=VMEM_LIMIT),
        cost_estimate=pl.CostEstimate(
            flops=4 * tokens * depth * wi, bytes_accessed=4 * depth * wi + 8 * tokens * wi, transcendentals=0
        ),
    )(place, mask, x, weight, *([] if more is None else [more]))


def apply_kernel(transposed, wi, first, place, mask, x_ref, w_ref, y_ref, *rest):
    if first:
        dw_ref, acc_ref = rest
    else:
        _, old_ref, dw_ref, acc_ref = rest
    q = pl.program_id(0)
    at = place[q] * (wi // BLOCK)

    @pl.when(q == 0)
    def _():
        acc_ref[...] = jnp.zeros_like(acc_ref) if first else old_ref[...]

    x = x_ref[0]
    if transposed:
        acc_ref[...] += contract(x, masked_block(w_ref, mask, 0, at), 1, 1)
        grad = contract(y_ref[...], x, 1, 0)
    else:
        acc_ref[...] += contract(x, masked_block(w_ref, mask, at, 0), 1, 0)
        grad = contract(x, y_ref[...], 0, 0)
    for i in range(grad.shape[0] // BLOCK):
        for j in range(grad.shape[1] // BLOCK):
            part = grad[i * BLOCK : (i + 1) * BLOCK, j * BLOCK : (j + 1) * BLOCK]
            there = mask[i, at + j] if transposed else mask[at + i, j]
            part = jnp.where(there > 0, part, jnp.zeros_like(part))
            dw_ref[i * BLOCK : (i + 1) * BLOCK, j * BLOCK : (j + 1) * BLOCK] = part.astype(dw_ref.dtype)


def apply_part(x, weight, mask, other, place, state, transposed):
    blocks, tokens, wi = x.shape
    first = state is None
    depth = weight.shape[0] if transposed else weight.shape[1]
    if transposed:
        wspec = pl.BlockSpec((depth, wi), lambda q, place, mask: (0, place[q]))
    else:
        wspec = pl.BlockSpec((wi, depth), lambda q, place, mask: (place[q], 0))
    whole = lambda shape: pl.BlockSpec(shape, lambda q, place, mask: (0,) * len(shape))
    in_specs = [pl.BlockSpec((1, tokens, wi), lambda q, place, mask: (q, 0, 0)), wspec, whole(other.shape)]
    args = [x, weight, other]
    aliases = {}
    if not first:
        in_specs += [pl.BlockSpec(memory_space=pl.ANY), whole((tokens, depth))]
        args += list(state)
        aliases = {5: 0, 6: 1}
    return pl.pallas_call(
        functools.partial(apply_kernel, transposed, wi, first),
        grid_spec=pltpu.PrefetchScalarGridSpec(
            num_scalar_prefetch=2,
            grid=(blocks,),
            in_specs=in_specs,
            out_specs=[wspec, whole((tokens, depth))],
        ),
        out_shape=[
            jax.ShapeDtypeStruct(weight.shape, weight.dtype),
            jax.ShapeDtypeStruct((tokens, depth), jnp.float32),
        ],
        input_output_aliases=aliases,
        compiler_params=pltpu.CompilerParams(vmem_limit_bytes=VMEM_LIMIT),
        cost_estimate=pl.CostEstimate(
            flops=4 * blocks * tokens * depth * wi,
            bytes_accessed=4 * blocks * depth * wi + 8 * tokens * depth,
            transcendentals=0,
        ),
    )(place, mask, *args)


def body(tokens, weight_in, mask_in, weight_out, mask_out, cotangent):
    n = CHUNKS
    rows, line = lax.axis_size("row"), lax.axis_size("col") // 2
    hidden_units = weight_in.shape[1]
    wi = hidden_units // (4 * n)
    here = lax.axis_index("col")
    z, core = here // 2, here % 2
    half, total = line // 2, 2 * n
    legs = half - 1
    last = []

    def after(x):
        return lax.optimization_barrier((x, last[0]))[0] if last else x

    def mark(x):
        last[:] = [x]
        return x

    def across_row(x, r):
        return lax.ppermute(x, "row", [(i, i ^ r) for i in range(rows)])

    def swap(x):
        return lax.ppermute(x, "col", [(i, i ^ 1) for i in range(2 * line)])

    def send_along(x, pairs):
        return lax.ppermute(x, "col", [(2 * p + k, 2 * q + k) for p, q in pairs for k in range(2)])

    def both_ends(p, q):
        return [(p, q), (line - 1 - p, line - 1 - q)]

    tokens_all = jnp.concatenate([tokens] + [across_row(tokens, r) for r in range(1, rows)], axis=0)
    cotangent_all = jnp.concatenate([cotangent] + [across_row(cotangent, r) for r in range(1, rows)], axis=0)
    tokens_t = tokens_all.T

    def place_of(chunk, side):
        return jnp.stack([chunk * 4 + d + 2 * side for d in range(2)])

    sent, sums = {}, {}

    def start_partial(k):
        x, w, m = (tokens_all, weight_in, mask_in) if k < n else (cotangent_all, weight_out, mask_out)
        term = partial_sums(x, w, m, after(place_of(k % n, 1 - core)), wi, k >= n)
        sent[k] = swap(mark(term))

    def end_partial(k):
        x, w, m = (tokens_all, weight_in, mask_in) if k < n else (cotangent_all, weight_out, mask_out)
        sums[k] = mark(partial_sums(x, w, m, after(place_of(k % n, core)), wi, k >= n, sent.pop(k)))

    lower = z < half
    preact, items, full, own, oth = {}, {}, {}, {}, {}
    outer, middle, kept = {}, {}, {}
    states = [None, None]

    def outer_step(s):
        for h in range(legs):
            inward, outward = s - h, s - (2 * legs + 1) + h
            pairs, choices = [], []
            if 0 <= inward < total:
                pairs += both_ends(h, h + 1)
                choices.append(sums[inward].astype(jnp.bfloat16))
            if 0 <= outward < total:
                pairs += both_ends(h + 1, h)
                choices.append(full[outward])
            if not pairs:
                continue
            sender = (z == h) | (z == line - 1 - h)
            x = choices[0] if len(choices) == 1 else jnp.where(sender, *choices)
            outer[s, h] = send_along(mark(after(x)), pairs)

    def outer_end(s):
        for h in range(legs):
            inward, outward = s - h, s - (2 * legs + 1) + h
            if (s, h) not in outer:
                continue
            got = outer.pop((s, h))
            if 0 <= inward < total:
                sums[inward] = sums[inward] + got.astype(jnp.float32)
            if 0 <= outward < total:
                here_now = (z == h) | (z == line - 1 - h)
                full[outward] = jnp.where(here_now, got, full[outward])

    def middle_step(s):
        b, c = s - legs, s - legs - 1
        parts = []
        if 0 <= b < total:
            total_sum = sums.pop(b)
            kept[b] = jnp.where(lower, total_sum[0], total_sum[1])
            parts.append(jnp.where(lower, total_sum[1], total_sum[0]).astype(jnp.bfloat16))
        if 0 <= c < total:
            parts.append(items[c])
        if parts:
            middle[s] = send_along(mark(after(jnp.stack(parts))), [(half - 1, half), (half, half - 1)])

    def middle_end(s):
        b, c = s - legs, s - legs - 1
        if s not in middle:
            return
        got = middle.pop(s)
        if 0 <= b < total:
            value = kept.pop(b) + got[0].astype(jnp.float32)
            if b < n:
                preact[b] = value
                item = gelu_value(value)
            else:
                item = value * gelu_slope(preact[b - n])
            items[b] = lax.optimization_barrier(item.astype(jnp.bfloat16))
        if 0 <= c < total:
            mine, other = items.pop(c), got[-1]
            full[c] = jnp.stack([jnp.where(lower, mine, other), jnp.where(lower, other, mine)])

    def collect(j):
        own[j] = mark(after(full.pop(j)))
        oth[j] = swap(own[j])

    def apply(j, mine):
        back = j >= n
        w, m, other = (weight_in, mask_in, tokens_t) if back else (weight_out, mask_out, cotangent_all)
        x = own.pop(j) if mine else oth.pop(j)
        place = after(place_of(j % n, core if mine else 1 - core))
        states[back] = mark(apply_part(x, w, m, other, place, states[back], back))

    def spread(total_sum):
        parts = total_sum.reshape(rows, total_sum.shape[0] // rows, total_sum.shape[1])
        out = parts[0]
        for r in range(1, rows):
            out = out + across_row(parts[r].astype(jnp.bfloat16), r).astype(jnp.float32)
        return out.astype(jnp.bfloat16)

    start_partial(0)
    start_partial(1)
    end_partial(0)
    last_step = total + 2 * legs + 1
    for s in range(last_step):
        outer_step(s)
        middle_step(s)
        ready = s - (2 * legs + 2)
        if ready >= 0:
            collect(ready)
        if s + 2 < total:
            start_partial(s + 2)
        if s + 1 < total:
            end_partial(s + 1)
        if ready >= 1:
            apply(ready - 1, True)
            apply(ready - 1, False)
        outer_end(s)
        middle_end(s)
    collect(total - 1)
    for j in (total - 2, total - 1):
        apply(j, True)
        apply(j, False)
    (weight_out_grad, result), (weight_in_grad, tokens_grad) = states
    return (spread(result), spread(tokens_grad), weight_in_grad, weight_out_grad)


def solution(mesh):
    return jax.shard_map(
        body,
        mesh=mesh,
        in_specs=(
            P("row", "col"),
            P("col", "row"),
            P("col", "row"),
            P("row", "col"),
            P("row", "col"),
            P("row", "col"),
        ),
        out_specs=(P("row", "col"), P("row", "col"), P("col", "row"), P("row", "col")),
        check_vma=False,
    )
```

```python
import functools

import jax
import jax.numpy as jnp
from jax import lax
from jax.experimental import pallas as pl
from jax.experimental.pallas import tpu as pltpu
from jax.sharding import PartitionSpec as P

BLOCK = 128
CHUNKS = 4
VMEM_LIMIT = 40 * 1024 * 1024

root_two_pi = 0.7978845608
cubic_coef = 0.044715


def gelu_value(values):
    tangent = jnp.tanh(root_two_pi * (values + cubic_coef * values * values * values))
    return 0.5 * values * (1.0 + tangent)


def gelu_slope(values):
    tangent = jnp.tanh(root_two_pi * (values + cubic_coef * values * values * values))
    return 0.5 * (1.0 + tangent) + 0.5 * values * (1.0 - tangent * tangent) * root_two_pi * (
        1.0 + 3.0 * cubic_coef * values * values
    )


def contract(left, right, left_dim, right_dim):
    return lax.dot_general(
        left, right, (((left_dim,), (right_dim,)), ((), ())), preferred_element_type=jnp.float32
    )


def masked_block(w_ref, mask_ref, row0, col0):
    rows, cols = w_ref.shape
    bands = []
    for i in range(rows // BLOCK):
        parts = []
        for j in range(cols // BLOCK):
            part = w_ref[i * BLOCK : (i + 1) * BLOCK, j * BLOCK : (j + 1) * BLOCK]
            parts.append(jnp.where(mask_ref[row0 + i, col0 + j] > 0, part, jnp.zeros_like(part)))
        bands.append(parts[0] if len(parts) == 1 else jnp.concatenate(parts, axis=1))
    return bands[0] if len(bands) == 1 else jnp.concatenate(bands, axis=0)


def partial_kernel(transposed, wi, place, mask, x_ref, w_ref, *rest):
    out_ref = rest[-1]
    at = place[pl.program_id(0)] * (wi // BLOCK)
    if transposed:
        term = contract(x_ref[...], masked_block(w_ref, mask, at, 0), 1, 1)
    else:
        term = contract(x_ref[...], masked_block(w_ref, mask, 0, at), 1, 0)
    if len(rest) > 1:
        term += rest[0][0]
    out_ref[0] = term


def partial_sums(x, weight, mask, place, wi, transposed, more=None):
    tokens, depth = x.shape
    if transposed:
        wspec = pl.BlockSpec((wi, depth), lambda d, place, mask: (place[d], 0))
    else:
        wspec = pl.BlockSpec((depth, wi), lambda d, place, mask: (0, place[d]))
    out_spec = pl.BlockSpec((1, tokens, wi), lambda d, place, mask: (d, 0, 0))
    return pl.pallas_call(
        functools.partial(partial_kernel, transposed, wi),
        grid_spec=pltpu.PrefetchScalarGridSpec(
            num_scalar_prefetch=2,
            grid=(2,),
            in_specs=[pl.BlockSpec((tokens, depth), lambda d, place, mask: (0, 0)), wspec] + [out_spec] * (more is not None),
            out_specs=out_spec,
        ),
        out_shape=jax.ShapeDtypeStruct((2, tokens, wi), jnp.float32),
        compiler_params=pltpu.CompilerParams(vmem_limit_bytes=VMEM_LIMIT),
        cost_estimate=pl.CostEstimate(flops=1024, bytes_accessed=1024, transcendentals=0),
    )(place, mask, x, weight, *([] if more is None else [more]))


def total_kernel(transposed, wi, first, place, mask, x_ref, w_ref, *rest):
    acc_ref = rest[-1]
    q = pl.program_id(0)

    @pl.when(q == 0)
    def _():
        acc_ref[...] = jnp.zeros_like(acc_ref) if first else rest[0][...]

    add_product(transposed, wi, place[q], mask, x_ref[0], w_ref, acc_ref)


def add_product(transposed, wi, block, mask, x, w_ref, acc_ref):
    at = block * (wi // BLOCK)
    if transposed:
        acc_ref[...] += contract(x, masked_block(w_ref, mask, 0, at), 1, 1)
    else:
        acc_ref[...] += contract(x, masked_block(w_ref, mask, at, 0), 1, 0)


def store_grad(transposed, wi, block, mask, x, y_ref, dw_ref):
    at = block * (wi // BLOCK)
    grad = contract(y_ref[...], x, 1, 0) if transposed else contract(x, y_ref[...], 0, 0)
    for i in range(grad.shape[0] // BLOCK):
        for j in range(grad.shape[1] // BLOCK):
            part = grad[i * BLOCK : (i + 1) * BLOCK, j * BLOCK : (j + 1) * BLOCK]
            there = mask[i, at + j] if transposed else mask[at + i, j]
            part = jnp.where(there > 0, part, jnp.zeros_like(part))
            dw_ref[i * BLOCK : (i + 1) * BLOCK, j * BLOCK : (j + 1) * BLOCK] = part.astype(dw_ref.dtype)


def grad_kernel(transposed, wi, place, mask, x_ref, y_ref, _, dw_ref):
    store_grad(transposed, wi, place[pl.program_id(0)], mask, x_ref[0], y_ref, dw_ref)


def apply_kernel(transposed, wi, first, place, mask, x_ref, w_ref, y_ref, *rest):
    dw_ref, acc_ref = rest[-2:]
    q = pl.program_id(0)

    @pl.when(q == 0)
    def _():
        acc_ref[...] = jnp.zeros_like(acc_ref) if first else rest[1][...]

    add_product(transposed, wi, place[q], mask, x_ref[0], w_ref, acc_ref)
    store_grad(transposed, wi, place[q], mask, x_ref[0], y_ref, dw_ref)


def apply_part(x, weight, mask, other, place, state, transposed, what="both"):
    blocks, tokens, wi = x.shape
    first = state is None
    depth = weight.shape[0] if transposed else weight.shape[1]
    if transposed:
        wspec = pl.BlockSpec((depth, wi), lambda q, place, mask: (0, place[q]))
    else:
        wspec = pl.BlockSpec((wi, depth), lambda q, place, mask: (place[q], 0))
    whole = lambda shape: pl.BlockSpec(shape, lambda q, place, mask: (0,) * len(shape))
    xspec = pl.BlockSpec((1, tokens, wi), lambda q, place, mask: (q, 0, 0))
    acc, dw = jax.ShapeDtypeStruct((tokens, depth), jnp.float32), jax.ShapeDtypeStruct(weight.shape, weight.dtype)
    anywhere, total = pl.BlockSpec(memory_space=pl.ANY), whole((tokens, depth))
    if what == "both":
        kernel = functools.partial(apply_kernel, transposed, wi, first)
        in_specs, args = [xspec, wspec, whole(other.shape)], [x, weight, other]
        out_specs, out_shape, aliases = [wspec, total], [dw, acc], {}
        if not first:
            in_specs, args, aliases = in_specs + [anywhere, total], args + list(state), {5: 0, 6: 1}
    elif what == "total":
        kernel = functools.partial(total_kernel, transposed, wi, first)
        in_specs, args = [xspec, wspec, total], [x, weight, state[1]]
        out_specs, out_shape, aliases = [total], [acc], {4: 0}
    else:
        kernel = functools.partial(grad_kernel, transposed, wi)
        in_specs, args = [xspec, whole(other.shape), anywhere], [x, other, state[0]]
        out_specs, out_shape, aliases = [wspec], [dw], {4: 0}
    return pl.pallas_call(
        kernel,
        grid_spec=pltpu.PrefetchScalarGridSpec(
            num_scalar_prefetch=2, grid=(blocks,), in_specs=in_specs, out_specs=out_specs
        ),
        out_shape=out_shape,
        input_output_aliases=aliases,
        compiler_params=pltpu.CompilerParams(vmem_limit_bytes=VMEM_LIMIT),
        cost_estimate=pl.CostEstimate(flops=1024, bytes_accessed=1024, transcendentals=0),
    )(place, mask, *args)


def body(tokens, weight_in, mask_in, weight_out, mask_out, cotangent):
    n = CHUNKS
    rows, line = lax.axis_size("row"), lax.axis_size("col") // 2
    hidden_units = weight_in.shape[1]
    wi = hidden_units // (4 * n)
    here = lax.axis_index("col")
    z, core = here // 2, here % 2
    half, total = line // 2, 2 * n
    legs = half - 1
    last = []

    def after(x):
        return lax.optimization_barrier((x, last[0]))[0] if last else x

    def mark(x):
        last[:] = [x]
        return x

    def across_row(x, r):
        return lax.ppermute(x, "row", [(i, i ^ r) for i in range(rows)])

    def swap(x):
        return lax.ppermute(x, "col", [(i, i ^ 1) for i in range(2 * line)])

    def send_along(x, pairs):
        return lax.ppermute(x, "col", [(2 * p + k, 2 * q + k) for p, q in pairs for k in range(2)])

    def both_ends(p, q):
        return [(p, q), (line - 1 - p, line - 1 - q)]

    tokens_all = jnp.concatenate([tokens] + [across_row(tokens, r) for r in range(1, rows)], axis=0)
    cotangent_all = [cotangent] + [across_row(cotangent, r) for r in range(1, rows)]
    tokens_t = tokens_all.T

    def place_of(chunk, side):
        return jnp.stack([chunk * 4 + d + 2 * side for d in range(2)])

    sent, sums = {}, {}

    def start_partial(k):
        x, w, m = (tokens_all, weight_in, mask_in) if k < n else (cotangent_all, weight_out, mask_out)
        term = partial_sums(x, w, m, after(place_of(k % n, 1 - core)), wi, k >= n)
        sent[k] = swap(mark(term))

    def end_partial(k):
        x, w, m = (tokens_all, weight_in, mask_in) if k < n else (cotangent_all, weight_out, mask_out)
        sums[k] = mark(partial_sums(x, w, m, after(place_of(k % n, core)), wi, k >= n, sent.pop(k)))

    lower = z < half
    preact, items, full, own, oth = {}, {}, {}, {}, {}
    outer, middle, kept = {}, {}, {}
    states = [None, None]

    def outer_step(s):
        for h in range(legs):
            inward, outward = s - h, s - (2 * legs + 1) + h
            pairs, choices = [], []
            if 0 <= inward < total:
                pairs += both_ends(h, h + 1)
                choices.append(sums[inward].astype(jnp.bfloat16))
            if 0 <= outward < total:
                pairs += both_ends(h + 1, h)
                choices.append(full[outward])
            if not pairs:
                continue
            sender = (z == h) | (z == line - 1 - h)
            if len(pairs) == 2 and legs == 1:
                pairs += [(q, p) for p, q in pairs]
            x = choices[0] if len(choices) == 1 else jnp.where(sender, *choices)
            outer[s, h] = send_along(mark(after(x)), pairs)

    def outer_end(s):
        for h in range(legs):
            inward, outward = s - h, s - (2 * legs + 1) + h
            if (s, h) not in outer:
                continue
            got = after(outer.pop((s, h)))
            if 0 <= inward < total:
                sums[inward] = sums[inward] + got.astype(jnp.float32)
            if 0 <= outward < total:
                here_now = (z == h) | (z == line - 1 - h)
                full[outward] = jnp.where(here_now, got, full[outward])

    def middle_step(s):
        b, c = s - legs, s - legs - 1
        parts = []
        if 0 <= b < total:
            total_sum = sums.pop(b)
            kept[b] = jnp.where(lower, total_sum[0], total_sum[1])
            parts.append(jnp.where(lower, total_sum[1], total_sum[0]).astype(jnp.bfloat16))
        if 0 <= c < total:
            parts.append(items[c])
        if parts:
            middle[s] = send_along(mark(after(jnp.stack(parts))), [(half - 1, half), (half, half - 1)])

    def middle_gathered(s):
        c = s - legs - 1
        if s in middle and 0 <= c < total:
            middle[s] = after(middle[s])
            mine, other = items.pop(c), middle[s][-1]
            full[c] = jnp.stack([jnp.where(lower, mine, other), jnp.where(lower, other, mine)])

    def middle_summed(s):
        b = s - legs
        if s in middle and 0 <= b < total:
            value = kept.pop(b) + after(middle.pop(s))[0].astype(jnp.float32)
            if b < n:
                preact[b] = value
                item = gelu_value(value)
            else:
                item = value * gelu_slope(preact[b - n])
            items[b] = lax.optimization_barrier(item.astype(jnp.bfloat16))

    def collect(j):
        own[j] = mark(after(full.pop(j)))
        oth[j] = swap(own[j])

    def apply(j, mine, what="both"):
        back = j >= n
        w, m, other = (weight_in, mask_in, tokens_t) if back else (weight_out, mask_out, cotangent_all)
        x = own[j] if mine else oth[j]
        place = after(place_of(j % n, core if mine else 1 - core))
        got = mark(apply_part(x, w, m, other, place, states[back], back, what))
        if what == "total":
            states[back] = (states[back][0], got[0])
        elif what == "gradient":
            states[back] = (got[0], states[back][1])
        else:
            states[back] = got

    def spread(total_sum):
        parts = mark(after(total_sum)).reshape(rows, total_sum.shape[0] // rows, total_sum.shape[1])
        out = parts[0]
        for r in range(1, rows):
            out = out + across_row(parts[r].astype(jnp.bfloat16), r).astype(jnp.float32)
        return out.astype(jnp.bfloat16)

    start_partial(0)
    start_partial(1)
    end_partial(0)
    result = None
    for s in range(total + 2 * legs + 1):
        if s > 1:
            outer_end(s - 1)
            middle_gathered(s - 1)
            middle_summed(s - 1)
            middle_step(s)
            outer_step(s)
        else:
            outer_step(s)
            outer_end(s - 1)
            middle_step(s)
        ready = s - (2 * legs + 2)
        if ready >= 0:
            collect(ready)
        if s == 0:
            cotangent_all = mark(after(jnp.concatenate(cotangent_all, axis=0)))
        if s + 2 < total:
            start_partial(s + 2)
        if s + 1 < total:
            end_partial(s + 1)
        if ready >= 0:
            apply(ready, True)
            apply(ready, False)
        if ready == n:
            result = mark(after(result))
        if ready == n - 1:
            result = spread(states[0][1])
    outer_end(total + 2 * legs)
    collect(total - 1)
    apply(total - 1, True, "total")
    apply(total - 1, False, "total")
    tokens_grad = spread(states[1][1])
    apply(total - 1, True, "gradient")
    apply(total - 1, False, "gradient")
    return (result, tokens_grad, states[1][0], states[0][0])


def solution(mesh):
    return jax.shard_map(
        body,
        mesh=mesh,
        in_specs=(
            P("row", "col"),
            P("col", "row"),
            P("col", "row"),
            P("row", "col"),
            P("row", "col"),
            P("row", "col"),
        ),
        out_specs=(P("row", "col"), P("row", "col"), P("col", "row"), P("row", "col")),
        check_vma=False,
    )
```

```python
import functools

import jax
import jax.numpy as jnp
from jax import lax
from jax.experimental import pallas as pl
from jax.experimental.pallas import tpu as pltpu
from jax.sharding import PartitionSpec as P

BLOCK = 128
CHUNKS = 4
VMEM_LIMIT = 24 * 1024 * 1024

root_two_pi = 0.7978845608
cubic_coef = 0.044715


def gelu_value(values):
    tangent = jnp.tanh(root_two_pi * (values + cubic_coef * values * values * values))
    return 0.5 * values * (1.0 + tangent)


def gelu_slope(values):
    tangent = jnp.tanh(root_two_pi * (values + cubic_coef * values * values * values))
    return 0.5 * (1.0 + tangent) + 0.5 * values * (1.0 - tangent * tangent) * root_two_pi * (
        1.0 + 3.0 * cubic_coef * values * values
    )


def contract(left, right, left_dim, right_dim):
    return lax.dot_general(
        left, right, (((left_dim,), (right_dim,)), ((), ())), preferred_element_type=jnp.float32
    )


def masked_block(w_ref, mask_ref, row0, col0):
    rows, cols = w_ref.shape
    bands = []
    for i in range(rows // BLOCK):
        parts = []
        for j in range(cols // BLOCK):
            part = w_ref[i * BLOCK : (i + 1) * BLOCK, j * BLOCK : (j + 1) * BLOCK]
            parts.append(jnp.where(mask_ref[row0 + i, col0 + j] > 0, part, jnp.zeros_like(part)))
        bands.append(parts[0] if len(parts) == 1 else jnp.concatenate(parts, axis=1))
    return bands[0] if len(bands) == 1 else jnp.concatenate(bands, axis=0)


def partial_kernel(transposed, wi, place, mask, x_ref, w_ref, *rest):
    out_ref = rest[-1]
    at = place[pl.program_id(0)] * (wi // BLOCK)
    if transposed:
        term = contract(x_ref[...], masked_block(w_ref, mask, at, 0), 1, 1)
    else:
        term = contract(x_ref[...], masked_block(w_ref, mask, 0, at), 1, 0)
    if len(rest) > 1:
        term += rest[0][0]
    out_ref[0] = term


def partial_sums(x, weight, mask, place, wi, transposed, more=None):
    tokens, depth = x.shape
    if transposed:
        wspec = pl.BlockSpec((wi, depth), lambda d, place, mask: (place[d], 0))
    else:
        wspec = pl.BlockSpec((depth, wi), lambda d, place, mask: (0, place[d]))
    out_spec = pl.BlockSpec((1, tokens, wi), lambda d, place, mask: (d, 0, 0))
    return pl.pallas_call(
        functools.partial(partial_kernel, transposed, wi),
        grid_spec=pltpu.PrefetchScalarGridSpec(
            num_scalar_prefetch=2,
            grid=(2,),
            in_specs=[pl.BlockSpec((tokens, depth), lambda d, place, mask: (0, 0)), wspec] + [out_spec] * (more is not None),
            out_specs=out_spec,
        ),
        out_shape=jax.ShapeDtypeStruct((2, tokens, wi), jnp.float32),
        compiler_params=pltpu.CompilerParams(vmem_limit_bytes=VMEM_LIMIT),
        cost_estimate=pl.CostEstimate(flops=1024, bytes_accessed=1024, transcendentals=0),
    )(place, mask, x, weight, *([] if more is None else [more]))


def total_kernel(transposed, wi, first, place, mask, x_ref, w_ref, *rest):
    acc_ref = rest[-1]
    q = pl.program_id(0)

    @pl.when(q == 0)
    def _():
        acc_ref[...] = jnp.zeros_like(acc_ref) if first else rest[0][...]

    add_product(transposed, wi, place[q], mask, x_ref[0], w_ref, acc_ref)


def add_product(transposed, wi, block, mask, x, w_ref, acc_ref):
    at = block * (wi // BLOCK)
    if transposed:
        acc_ref[...] += contract(x, masked_block(w_ref, mask, 0, at), 1, 1)
    else:
        acc_ref[...] += contract(x, masked_block(w_ref, mask, at, 0), 1, 0)


def store_grad(transposed, wi, block, mask, x, y_ref, dw_ref):
    at = block * (wi // BLOCK)
    grad = contract(y_ref[...], x, 1, 0) if transposed else contract(x, y_ref[...], 0, 0)
    for i in range(grad.shape[0] // BLOCK):
        for j in range(grad.shape[1] // BLOCK):
            part = grad[i * BLOCK : (i + 1) * BLOCK, j * BLOCK : (j + 1) * BLOCK]
            there = mask[i, at + j] if transposed else mask[at + i, j]
            part = jnp.where(there > 0, part, jnp.zeros_like(part))
            dw_ref[i * BLOCK : (i + 1) * BLOCK, j * BLOCK : (j + 1) * BLOCK] = part.astype(dw_ref.dtype)


def grad_kernel(transposed, wi, place, mask, x_ref, y_ref, _, dw_ref):
    store_grad(transposed, wi, place[pl.program_id(0)], mask, x_ref[0], y_ref, dw_ref)


def apply_kernel(transposed, wi, first, place, mask, x_ref, w_ref, y_ref, *rest):
    dw_ref, acc_ref = rest[-2:]
    q = pl.program_id(0)

    @pl.when(q == 0)
    def _():
        acc_ref[...] = jnp.zeros_like(acc_ref) if first else rest[1][...]

    add_product(transposed, wi, place[q], mask, x_ref[0], w_ref, acc_ref)
    store_grad(transposed, wi, place[q], mask, x_ref[0], y_ref, dw_ref)


def apply_part(x, weight, mask, other, place, state, transposed, what="both"):
    blocks, tokens, wi = x.shape
    first = state is None
    depth = weight.shape[0] if transposed else weight.shape[1]
    if transposed:
        wspec = pl.BlockSpec((depth, wi), lambda q, place, mask: (0, place[q]))
    else:
        wspec = pl.BlockSpec((wi, depth), lambda q, place, mask: (place[q], 0))
    whole = lambda shape: pl.BlockSpec(shape, lambda q, place, mask: (0,) * len(shape))
    xspec = pl.BlockSpec((1, tokens, wi), lambda q, place, mask: (q, 0, 0))
    acc, dw = jax.ShapeDtypeStruct((tokens, depth), jnp.float32), jax.ShapeDtypeStruct(weight.shape, weight.dtype)
    anywhere, total = pl.BlockSpec(memory_space=pl.ANY), whole((tokens, depth))
    if what == "both":
        kernel = functools.partial(apply_kernel, transposed, wi, first)
        in_specs, args = [xspec, wspec, whole(other.shape)], [x, weight, other]
        out_specs, out_shape, aliases = [wspec, total], [dw, acc], {}
        if not first:
            in_specs, args, aliases = in_specs + [anywhere, total], args + list(state), {5: 0, 6: 1}
    elif what == "total":
        kernel = functools.partial(total_kernel, transposed, wi, first)
        in_specs, args = [xspec, wspec, total], [x, weight, state[1]]
        out_specs, out_shape, aliases = [total], [acc], {4: 0}
    else:
        kernel = functools.partial(grad_kernel, transposed, wi)
        in_specs, args = [xspec, whole(other.shape), anywhere], [x, other, state[0]]
        out_specs, out_shape, aliases = [wspec], [dw], {4: 0}
    return pl.pallas_call(
        kernel,
        grid_spec=pltpu.PrefetchScalarGridSpec(
            num_scalar_prefetch=2, grid=(blocks,), in_specs=in_specs, out_specs=out_specs
        ),
        out_shape=out_shape,
        input_output_aliases=aliases,
        compiler_params=pltpu.CompilerParams(vmem_limit_bytes=VMEM_LIMIT),
        cost_estimate=pl.CostEstimate(flops=1024, bytes_accessed=1024, transcendentals=0),
    )(place, mask, *args)


def body(tokens, weight_in, mask_in, weight_out, mask_out, cotangent):
    n = CHUNKS
    rows, line = lax.axis_size("row"), lax.axis_size("col") // 2
    hidden_units = weight_in.shape[1]
    wi = hidden_units // (4 * n)
    here = lax.axis_index("col")
    z, core = here // 2, here % 2
    half, total = line // 2, 2 * n
    legs = half - 1
    last = []

    def after(x):
        return lax.optimization_barrier((x, last[0]))[0] if last else x

    def mark(x):
        last[:] = [x]
        return x

    def across_row(x, r):
        return lax.ppermute(x, "row", [(i, i ^ r) for i in range(rows)])

    def swap(x):
        return lax.ppermute(x, "col", [(i, i ^ 1) for i in range(2 * line)])

    def send_along(x, pairs):
        return lax.ppermute(x, "col", [(2 * p + k, 2 * q + k) for p, q in pairs for k in range(2)])

    def both_ends(p, q):
        return [(p, q), (line - 1 - p, line - 1 - q)]

    tokens_all = jnp.concatenate([tokens] + [across_row(tokens, r) for r in range(1, rows)], axis=0)
    cotangent_all = [cotangent] + [across_row(cotangent, r) for r in range(1, rows)]
    tokens_t = tokens_all.T

    def place_of(chunk, side):
        return jnp.stack([chunk * 4 + d + 2 * side for d in range(2)])

    sent, sums = {}, {}

    def start_partial(k):
        x, w, m = (tokens_all, weight_in, mask_in) if k < n else (cotangent_all, weight_out, mask_out)
        term = partial_sums(x, w, m, after(place_of(k % n, 1 - core)), wi, k >= n)
        sent[k] = swap(mark(term))

    def end_partial(k):
        x, w, m = (tokens_all, weight_in, mask_in) if k < n else (cotangent_all, weight_out, mask_out)
        sums[k] = mark(partial_sums(x, w, m, after(place_of(k % n, core)), wi, k >= n, sent.pop(k)))

    lower = z < half
    preact, items, full, own, oth = {}, {}, {}, {}, {}
    outer, middle, kept = {}, {}, {}
    states = [None, None]

    def outer_step(s):
        for h in range(legs):
            inward, outward = s - h, s - (2 * legs + 1) + h
            pairs, choices = [], []
            if 0 <= inward < total:
                pairs += both_ends(h, h + 1)
                choices.append(sums[inward].astype(jnp.bfloat16))
            if 0 <= outward < total:
                pairs += both_ends(h + 1, h)
                choices.append(full[outward])
            if not pairs:
                continue
            sender = (z == h) | (z == line - 1 - h)
            if len(pairs) == 2 and legs == 1:
                pairs += [(q, p) for p, q in pairs]
            x = choices[0] if len(choices) == 1 else jnp.where(sender, *choices)
            outer[s, h] = send_along(mark(after(x)), pairs)

    def outer_end(s):
        for h in range(legs):
            inward, outward = s - h, s - (2 * legs + 1) + h
            if (s, h) not in outer:
                continue
            got = after(outer.pop((s, h)))
            if 0 <= inward < total:
                sums[inward] = sums[inward] + got.astype(jnp.float32)
            if 0 <= outward < total:
                here_now = (z == h) | (z == line - 1 - h)
                full[outward] = jnp.where(here_now, got, full[outward])

    def middle_step(s):
        b, c = s - legs, s - legs - 1
        parts = []
        if 0 <= b < total:
            total_sum = sums.pop(b)
            kept[b] = jnp.where(lower, total_sum[0], total_sum[1])
            parts.append(jnp.where(lower, total_sum[1], total_sum[0]).astype(jnp.bfloat16))
        if 0 <= c < total:
            parts.append(items[c])
        if parts:
            middle[s] = send_along(mark(after(jnp.stack(parts))), [(half - 1, half), (half, half - 1)])

    def middle_gathered(s):
        c = s - legs - 1
        if s in middle and 0 <= c < total:
            middle[s] = after(middle[s])
            mine, other = items.pop(c), middle[s][-1]
            full[c] = jnp.stack([jnp.where(lower, mine, other), jnp.where(lower, other, mine)])

    def middle_summed(s):
        b = s - legs
        if s in middle and 0 <= b < total:
            value = kept.pop(b) + after(middle.pop(s))[0].astype(jnp.float32)
            if b < n:
                preact[b] = value
                item = gelu_value(value)
            else:
                item = value * gelu_slope(preact[b - n])
            items[b] = lax.optimization_barrier(item.astype(jnp.bfloat16))

    def collect(j):
        own[j] = mark(after(full.pop(j)))
        oth[j] = swap(own[j])

    def apply(j, mine, what="both"):
        back = j >= n
        w, m, other = (weight_in, mask_in, tokens_t) if back else (weight_out, mask_out, cotangent_all)
        x = own[j] if mine else oth[j]
        place = after(place_of(j % n, core if mine else 1 - core))
        got = mark(apply_part(x, w, m, other, place, states[back], back, what))
        if what == "total":
            states[back] = (states[back][0], got[0])
        elif what == "gradient":
            states[back] = (got[0], states[back][1])
        else:
            states[back] = got

    def spread(total_sum):
        parts = mark(after(total_sum)).reshape(rows, total_sum.shape[0] // rows, total_sum.shape[1])
        out = parts[0]
        for r in range(1, rows):
            out = out + across_row(parts[r].astype(jnp.bfloat16), r).astype(jnp.float32)
        return out.astype(jnp.bfloat16)

    start_partial(0)
    start_partial(1)
    end_partial(0)
    result = None
    for s in range(total + 2 * legs + 1):
        if s > 1:
            outer_end(s - 1)
            middle_gathered(s - 1)
            middle_summed(s - 1)
            middle_step(s)
            outer_step(s)
        else:
            outer_step(s)
            outer_end(s - 1)
            middle_step(s)
        ready = s - (2 * legs + 2)
        if ready >= 0:
            collect(ready)
        if s == 0:
            cotangent_all = mark(after(jnp.concatenate(cotangent_all, axis=0)))
        if s + 2 < total:
            start_partial(s + 2)
        if s + 1 < total:
            end_partial(s + 1)
        if ready >= 0:
            apply(ready, True)
            apply(ready, False)
        if ready == n:
            result = mark(after(result))
        if ready == n - 1:
            result = spread(states[0][1])
    outer_end(total + 2 * legs)
    collect(total - 1)
    apply(total - 1, True, "total")
    apply(total - 1, False, "total")
    tokens_grad = spread(states[1][1])
    apply(total - 1, True, "gradient")
    apply(total - 1, False, "gradient")
    return (result, tokens_grad, states[1][0], states[0][0])


def solution(mesh):
    return jax.shard_map(
        body,
        mesh=mesh,
        in_specs=(
            P("row", "col"),
            P("col", "row"),
            P("col", "row"),
            P("row", "col"),
            P("row", "col"),
            P("row", "col"),
        ),
        out_specs=(P("row", "col"), P("row", "col"), P("col", "row"), P("row", "col")),
        check_vma=False,
    )
```
